256 devices in a mesh: gx: 16 (over z, core), gy: 8 (over y, x_hi), gz: 2 (over x_lo).
Axes of the slice: x: 4 (x_hi: 2, x_lo: 2; x = x_hi * 2 + x_lo), y: 4, z: 8, core: 2. Of those that a mesh axis runs over, the one named last changes fastest.
Arguments:
- subspace: bfloat16 [4, 128, 128, 64, 128], P(None, 'gx', 'gy', 'gz'), may hold values from -100 to 100, as said below
- potential: float32 [128, 128, 64], P('gx', 'gy', 'gz'), may hold values from 0.09 to 11, as said below
Outputs:
- ortho_basis: bfloat16 [4, 128, 128, 64, 128], P(None, 'gx', 'gy', 'gz')
- ortho_image: bfloat16 [4, 128, 128, 64, 128], P(None, 'gx', 'gy', 'gz')
- reduced_matrix: float32 [4, 128, 128], replicated
- gram_first: float32 [4, 128, 128], replicated
The draws below stay inside these ranges and needn't reach their ends.
Inputs may be any that keep to these rules, and one draw needn't show every extreme that they name: `subspace`: entries are finite; the vectors of every interval are linearly independent. `potential`: positive everywhere.
All inputs are finite; a program needn't handle non-finite values.
Results may differ from the reference program's by a relative error of at most 0.0014.
The reference program's roundings to bfloat16 on the way (of `factor_one` and `applied`) count: a program that leaves them out, or rounds other values in their place, can miss the bound.
Values may be sent and summed in bfloat16 or wider, within the bound.
A program may use at most 64 MiB of HBM per device.

```python
import jax
import jax.numpy as jnp
from jax import lax

INTERVALS = 4
VECS = 128
NX = 128
NY = 128
NZ = 64


def draw_subspace(key, part):
    key = jax.random.fold_in(key, 11)
    keys = jax.random.split(key, 5)
    shape = (INTERVALS, NX, NY, NZ, VECS)
    noise = jnp.clip(jax.random.normal(keys[0], shape, jnp.float32), -4.0, 4.0)
    common = jnp.clip(jax.random.normal(keys[1], (1, NX, NY, NZ, 1), jnp.float32), -4.0, 4.0)
    coeff = jnp.clip(jax.random.normal(keys[2], (INTERVALS, 1, 1, 1, VECS), jnp.float32), -4.0, 4.0)
    share = 0.6
    rise = 3.0
    cell_scale = jnp.exp(jax.random.uniform(keys[3], (1, NX, NY, NZ, 1), jnp.float32, 0.0, jnp.log(10.0)))
    vec_scale = jnp.exp(jax.random.uniform(keys[4], (INTERVALS, 1, 1, 1, VECS), jnp.float32, 0.0, jnp.log(10.0)))
    position = jnp.arange(NX, dtype=jnp.float32).reshape(1, NX, 1, 1, 1) / max(NX - 1, 1)
    growth = jnp.exp(jnp.log(rise) * position)
    mixed = noise + share * common * coeff
    return jnp.clip(0.05 * mixed * cell_scale * vec_scale * growth, -100.0, 100.0).astype(jnp.bfloat16)


def draw_potential(key, part):
    key = jax.random.fold_in(key, 23)
    keys = jax.random.split(key, 2)
    strength = jnp.exp(jax.random.uniform(keys[0], (), jnp.float32, -1.0, 1.0))
    rough = jnp.exp(jax.random.uniform(keys[1], (NX, NY, NZ), jnp.float32, jnp.log(0.25), jnp.log(4.0)))
    return jnp.clip(strength * rough, 0.09, 11.0)


def setup_inputs(seed: int = 0) -> dict:
    seeds = jax.random.split(jax.random.key(seed), 3)
    return {
        "subspace": draw_subspace(jax.random.fold_in(seeds[2], 71), 0),
        "potential": draw_potential(jax.random.fold_in(seeds[2], 71), 0),
    }


def apply_ham(field, potential):
    padded = jnp.pad(field, ((1, 1), (1, 1), (1, 1), (0, 0)))
    center = padded[1:-1, 1:-1, 1:-1, :].astype(jnp.float32)
    beside = padded[2:, 1:-1, 1:-1, :].astype(jnp.float32) + padded[:-2, 1:-1, 1:-1, :].astype(jnp.float32)
    beside = beside + padded[1:-1, 2:, 1:-1, :].astype(jnp.float32)
    beside = beside + padded[1:-1, :-2, 1:-1, :].astype(jnp.float32)
    beside = beside + padded[1:-1, 1:-1, 2:, :].astype(jnp.float32)
    beside = beside + padded[1:-1, 1:-1, :-2, :].astype(jnp.float32)
    return ((6.0 + potential[..., None]) * center - beside).astype(jnp.bfloat16)

def inverse_factor(gram):
    lower = jnp.linalg.cholesky(gram)
    eye = jnp.eye(gram.shape[0], dtype=gram.dtype)
    return lax.linalg.triangular_solve(lower, eye, left_side=True, lower=True)

def pair_gram(left, right):
    return jnp.dot(left.astype(jnp.float32).T, right.astype(jnp.float32), precision=lax.Precision.HIGHEST)

def one_interval(block, potential):
    cells = block.shape[0] * block.shape[1] * block.shape[2]
    vectors = block.shape[3]
    flat = block.reshape(cells, vectors)
    gram_one = pair_gram(flat, flat) / cells
    factor_one = inverse_factor(gram_one).astype(jnp.bfloat16)
    applied = apply_ham(block, potential).reshape(cells, vectors)
    first_basis = jnp.dot(flat.astype(jnp.float32), factor_one.T.astype(jnp.float32), preferred_element_type=jnp.float32).astype(jnp.bfloat16)
    first_image = jnp.dot(applied.astype(jnp.float32), factor_one.T.astype(jnp.float32), preferred_element_type=jnp.float32).astype(jnp.bfloat16)
    gram_two = pair_gram(first_basis, first_basis) / cells
    crossed = pair_gram(first_basis, first_image) / cells
    projected = (crossed + crossed.T) * 0.5
    factor_two = inverse_factor(gram_two)
    factor_two_b = factor_two.astype(jnp.bfloat16)
    ortho_basis = jnp.dot(first_basis.astype(jnp.float32), factor_two_b.T.astype(jnp.float32), preferred_element_type=jnp.float32).astype(jnp.bfloat16)
    ortho_image = jnp.dot(first_image.astype(jnp.float32), factor_two_b.T.astype(jnp.float32), preferred_element_type=jnp.float32).astype(jnp.bfloat16)
    reduced = jnp.dot(jnp.dot(factor_two, projected, precision=lax.Precision.HIGHEST), factor_two.T, precision=lax.Precision.HIGHEST)
    return (ortho_basis.reshape(block.shape), ortho_image.reshape(block.shape), reduced, gram_one)

def reference(subspace, potential):
    ortho_basis, ortho_image, reduced_matrix, gram_first = lax.map(lambda block: one_interval(block, potential), subspace)
    return (ortho_basis, ortho_image, reduced_matrix, gram_first)
```

```python
import functools

import jax
import jax.numpy as jnp
from jax import lax
from jax.experimental import pallas as pl
from jax.experimental.pallas import tpu as pltpu
from jax.sharding import PartitionSpec as P

MESH = pl.DeviceIdType.MESH

def sum_kernel(x_ref, o_ref, got_one, got_two, send_one, recv_one, send_two, recv_two, send_three, recv_three):
    a, b, c = lax.axis_index("gx"), lax.axis_index("gy"), lax.axis_index("gz")
    na, nb, nc = lax.axis_size("gx"), lax.axis_size("gy"), lax.axis_size("gz")
    plane = nb * nc
    me = b * nc + c

    def in_plane(d):
        m = lax.rem(me + d, plane)
        return m, (a, m // nc, lax.rem(m, nc))

    def on_line(d):
        q = lax.rem(a + d, na)
        return q, (q, b, c)

    barrier = pltpu.get_barrier_semaphore()
    for d in range(1, plane):
        pl.semaphore_signal(barrier, inc=1, device_id=in_plane(d)[1], device_id_type=MESH)
    for d in range(1, na):
        pl.semaphore_signal(barrier, inc=1, device_id=on_line(d)[1], device_id_type=MESH)
    pl.semaphore_wait(barrier, plane + na - 2)

    def first(d):
        m, dev = in_plane(d)
        return pltpu.make_async_remote_copy(src_ref=x_ref.at[m], dst_ref=got_one.at[d], send_sem=send_one.at[d], recv_sem=recv_one.at[d], device_id=dev, device_id_type=MESH)

    def second(d):
        _, dev = on_line(d)
        return pltpu.make_async_remote_copy(src_ref=got_two.at[a], dst_ref=got_two.at[a], send_sem=send_two.at[d], recv_sem=recv_two.at[d], device_id=dev, device_id_type=MESH)

    def third(d):
        _, dev = in_plane(d)
        return pltpu.make_async_remote_copy(src_ref=o_ref.at[me], dst_ref=o_ref.at[me], send_sem=send_three.at[d], recv_sem=recv_three.at[d], device_id=dev, device_id_type=MESH)

    ones = [first(d) for d in range(1, plane)]
    for copy in ones:
        copy.start()
    for copy in ones:
        copy.wait_recv()
    total = x_ref[me]
    for d in range(1, plane):
        total = total + got_one[d]
    got_two[a] = total
    twos = [second(d) for d in range(1, na)]
    for copy in twos:
        copy.start()
    for copy in twos:
        copy.wait_recv()
    total = got_two[0]
    for q in range(1, na):
        total = total + got_two[q]
    o_ref[me] = total
    threes = [third(d) for d in range(1, plane)]
    for copy in threes:
        copy.start()
    for copy in threes:
        copy.wait_recv()
    for copy in ones + twos + threes:
        copy.wait_send()

def all_sum(x):
    chunks, rows, lanes = x.shape
    na = lax.axis_size("gx")
    dma = pltpu.SemaphoreType.DMA
    return pl.pallas_call(
        sum_kernel,
        out_shape=jax.ShapeDtypeStruct(x.shape, x.dtype),
        in_specs=[pl.BlockSpec(memory_space=pltpu.VMEM)],
        out_specs=pl.BlockSpec(memory_space=pltpu.VMEM),
        scratch_shapes=[
            pltpu.VMEM((chunks, rows, lanes), x.dtype),
            pltpu.VMEM((na, rows, lanes), x.dtype),
            dma((chunks,)), dma((chunks,)), dma((na,)), dma((na,)), dma((chunks,)), dma((chunks,)),
        ],
        compiler_params=pltpu.CompilerParams(collective_id=0, has_side_effects=True, vmem_limit_bytes=40 << 20),
    )(x)


V = 128
HI = lax.Precision.HIGHEST

def dotf(a, b, dims, precision=HI):
    return lax.dot_general(a, b, (dims, ((), ())), precision=precision, preferred_element_type=jnp.float32)

def eliminate(mats, width):
    n = len(mats)
    lane = lax.broadcasted_iota(jnp.int32, (width, V), 1)
    sub = lax.broadcasted_iota(jnp.int32, (width, V), 0)
    rows_out = [[] for _ in range(n)]
    mats = list(mats)
    for start in range(0, V, width):
        panels = [m[start:start + width] for m in mats]
        for j in range(width):
            here = start + j
            lo = (j + 1) // 8 * 8
            if j + 1 >= width:
                break
            for k in range(n):
                p = panels[k]
                row = p[j:j + 1, :]
                inv = 1.0 / row[:, here:here + 1]
                low = p[lo:]
                f = low[:, here:here + 1] * inv
                f = jnp.where(sub[lo:] > j, f, 0.0)
                f = jnp.broadcast_to(f, low.shape)
                new = jnp.where((lane[lo:] == here) & (sub[lo:] > j), -f, low - f * row)
                panels[k] = jnp.concatenate([p[:lo], new], axis=0) if lo else new
        for k in range(n):
            rows_out[k].append(panels[k])
        stop = start + width
        if stop < V:
            for k in range(n):
                p = panels[k]
                eye = lane == sub + start
                diag = jnp.sum(jnp.where(eye, p, 0.0), axis=1, keepdims=True)
                left = jnp.where(lane >= stop, p / diag, 0.0)
                upper = (lane > sub + start) & (lane < stop)
                right = jnp.where(upper, 0.0, jnp.where(eye, 1.0, p))
                m = mats[k][stop:]
                ln = lax.broadcasted_iota(jnp.int32, m.shape, 1)
                m = jnp.where((ln >= start) & (ln < stop), 0.0, m)
                upd = dotf(left, right, ((0,), (0,)))[stop:]
                mats[k] = jnp.concatenate([mats[k][:stop], m - upd], axis=0)
    return [jnp.concatenate(r, axis=0) for r in rows_out]

def factors(grams, width=32):
    lane = lax.broadcasted_iota(jnp.int32, (V, V), 1)
    sub = lax.broadcasted_iota(jnp.int32, (V, V), 0)
    eye = jnp.where(lane == sub, 1.0, 0.0)
    done = eliminate(grams, width)
    one, two, full = [], [], []
    for m in done:
        diag = jnp.sum(jnp.where(lane == sub, m, 0.0), axis=1, keepdims=True)
        scale = lax.rsqrt(diag)
        f = scale * jnp.where(lane < sub, m, eye)
        lt = scale * jnp.where(lane >= sub, m, 0.0)
        fb = f.astype(jnp.bfloat16)
        delta = fb.astype(jnp.float32) - f
        l2 = eye + dotf(delta, lt, ((1,), (1,)))
        l2 = jnp.where(lane <= sub, l2, 0.0)
        one.append(fb); full.append(f); two.append(l2)
    invs = []
    for l2 in two:
        diag = jnp.sum(jnp.where(lane == sub, l2, 0.0), axis=1, keepdims=True)
        invs.append(eye / diag)
    s = 1
    while s < V:
        pick = (lane // (2 * s) == sub // (2 * s)) & (lane // s != sub // s) & (lane < sub)
        t = [dotf(jnp.where(pick, l2, 0.0), x, ((1,), (0,))) for l2, x in zip(two, invs)]
        invs = [x - dotf(x, y, ((1,), (0,))) for x, y in zip(invs, t)]
        s *= 2
    return full, one, invs

def kernel(g_ref, s_ref, f1_ref, f2_ref, red_ref, width):
    grams = [g_ref[k] for k in range(4)]
    full, one, invs = factors(grams, width)
    for k in range(4):
        f1_ref[k] = one[k]
        f2_ref[k] = invs[k].astype(jnp.bfloat16)
        half = dotf(full[k], s_ref[k], ((1,), (0,)))
        red_ref[k] = dotf(half, full[k], ((1,), (1,)))

def small(g, s, width=32):
    return pl.pallas_call(
        functools.partial(kernel, width=width),
        out_shape=(jax.ShapeDtypeStruct((4, V, V), jnp.bfloat16), jax.ShapeDtypeStruct((4, V, V), jnp.bfloat16), jax.ShapeDtypeStruct((4, V, V), jnp.float32)),
        in_specs=[pl.BlockSpec(memory_space=pltpu.VMEM)] * 2,
        out_specs=(pl.BlockSpec(memory_space=pltpu.VMEM),) * 3,
        compiler_params=pltpu.CompilerParams(vmem_limit_bytes=40 << 20),
    )(g, s)


def with_halo(block, sides, width):
    for axis, dim in sides:
        count = lax.axis_size(axis)
        forward = [(i, i + 1) for i in range(count - 1)]
        backward = [(target, source) for source, target in forward]
        low = lax.ppermute(
            lax.slice_in_dim(block, block.shape[dim] - width, None, axis=dim), axis, forward
        )
        high = lax.ppermute(lax.slice_in_dim(block, 0, width, axis=dim), axis, backward)
        block = jnp.concatenate([low, block, high], axis=dim)
    return block


def apply_ham(padded, potential):
    center = padded[..., 1:-1, 1:-1, 1:-1, :].astype(jnp.float32)
    beside = padded[..., 2:, 1:-1, 1:-1, :].astype(jnp.float32) + padded[
        ..., :-2, 1:-1, 1:-1, :
    ].astype(jnp.float32)
    beside = beside + padded[..., 1:-1, 2:, 1:-1, :].astype(jnp.float32)
    beside = beside + padded[..., 1:-1, :-2, 1:-1, :].astype(jnp.float32)
    beside = beside + padded[..., 1:-1, 1:-1, 2:, :].astype(jnp.float32)
    beside = beside + padded[..., 1:-1, 1:-1, :-2, :].astype(jnp.float32)
    return ((6.0 + potential[..., None]) * center - beside).astype(jnp.bfloat16)


def batch_gram(left, right):
    return lax.dot_general(
        left, right, (((1,), (1,)), ((0,), (0,))), preferred_element_type=jnp.float32
    )


def batch_apply(factor, rows):
    return lax.dot_general(
        rows, factor, (((2,), (2,)), ((0,), (0,))), preferred_element_type=jnp.float32
    )


def per_device(subspace, potential):
    intervals = subspace.shape[0]
    brick = subspace.shape[1:4]
    vectors = subspace.shape[4]
    local_cells = brick[0] * brick[1] * brick[2]
    cells_total = local_cells * lax.axis_size("gx") * lax.axis_size("gy") * lax.axis_size("gz")
    flat = subspace.reshape(intervals, local_cells, vectors)
    padded = with_halo(subspace, (("gx", 1), ("gy", 2), ("gz", 3)), 1)
    applied = apply_ham(padded, potential)
    applied = applied.reshape(intervals, local_cells, vectors)
    partial = jnp.concatenate([batch_gram(flat, flat), batch_gram(flat, applied)])
    plane = lax.axis_size("gy") * lax.axis_size("gz")
    total = all_sum(partial.reshape(plane, -1, vectors)).reshape(partial.shape) / cells_total
    gram_one, crossed = total[:intervals], total[intervals:]
    crossed = (crossed + jnp.swapaxes(crossed, 1, 2)) * 0.5
    factor_one, factor_two, reduced_matrix = small(gram_one, crossed)
    first_basis = batch_apply(factor_one, flat).astype(jnp.bfloat16)
    first_image = batch_apply(factor_one, applied).astype(jnp.bfloat16)
    ortho_basis = batch_apply(factor_two, first_basis).astype(jnp.bfloat16)
    ortho_image = batch_apply(factor_two, first_image).astype(jnp.bfloat16)
    return (
        ortho_basis.reshape(subspace.shape),
        ortho_image.reshape(subspace.shape),
        reduced_matrix,
        gram_one,
    )


def solution(mesh):
    return jax.shard_map(
        per_device,
        mesh=mesh,
        in_specs=(P(None, "gx", "gy", "gz", None), P("gx", "gy", "gz")),
        out_specs=(P(None, "gx", "gy", "gz", None), P(None, "gx", "gy", "gz", None), P(), P()),
        check_vma=False,
    )
```

```python
import functools

import jax
import jax.numpy as jnp
from jax import lax
from jax.experimental import pallas as pl
from jax.experimental.pallas import tpu as pltpu
from jax.sharding import PartitionSpec as P

MESH = pl.DeviceIdType.MESH
HIGHEST = lax.Precision.HIGHEST
BF16 = jnp.bfloat16
F32 = jnp.float32
V = 128
K = 4
BX, BY, BZ = 8, 16, 32
CHUNK = 17


def dotf(a, b, dims):
    return lax.dot_general(a, b, (dims, ((), ())), precision=HIGHEST, preferred_element_type=F32)


def square_iotas():
    shape = (V, V)
    return lax.broadcasted_iota(jnp.int32, shape, 1), lax.broadcasted_iota(jnp.int32, shape, 0)


def eliminate(mats, width, after_panel):
    n = len(mats)
    lane = lax.broadcasted_iota(jnp.int32, (width, V), 1)
    sub = lax.broadcasted_iota(jnp.int32, (width, V), 0)
    done = [[] for _ in range(n)]
    mats = list(mats)
    for start in range(0, V, width):
        panels = [m[start : start + width] for m in mats]
        for j in range(width - 1):
            here = start + j
            lo = (j + 1) // 8 * 8
            for k in range(n):
                p = panels[k]
                row = p[j : j + 1, :]
                inv = 1.0 / row[:, here : here + 1]
                low = p[lo:]
                below = sub[lo:] > j
                f = jnp.where(below, low[:, here : here + 1] * inv, 0.0)
                new = jnp.where((lane[lo:] == here) & below, -f, low - f * row)
                panels[k] = jnp.concatenate([p[:lo], new], axis=0) if lo else new
        for k in range(n):
            done[k].append(panels[k])
        stop = start + width
        if stop < V:
            for k in range(n):
                p = panels[k]
                eye = lane == sub + start
                diag = jnp.sum(jnp.where(eye, p, 0.0), axis=1, keepdims=True)
                left = jnp.where(lane >= stop, p / diag, 0.0)
                upper = (lane > sub + start) & (lane < stop)
                right = jnp.where(upper, 0.0, jnp.where(eye, 1.0, p))
                m = mats[k][stop:]
                ln = lax.broadcasted_iota(jnp.int32, m.shape, 1)
                m = jnp.where((ln >= start) & (ln < stop), 0.0, m)
                update = dotf(left, right, ((0,), (0,)))[stop:]
                mats[k] = jnp.concatenate([mats[k][:stop], m - update], axis=0)
        after_panel(start // width)
    return [jnp.concatenate(rows, axis=0) for rows in done]


def factors(grams, after_panel):
    lane, sub = square_iotas()
    eye = jnp.where(lane == sub, 1.0, 0.0)
    full, one, two, invs = [], [], [], []
    for m in eliminate(grams, 32, after_panel):
        diag = jnp.sum(jnp.where(lane == sub, m, 0.0), axis=1, keepdims=True)
        scale = lax.rsqrt(diag)
        f = scale * jnp.where(lane < sub, m, eye)
        upper = scale * jnp.where(lane >= sub, m, 0.0)
        fb = f.astype(BF16)
        second = eye + dotf(fb.astype(F32) - f, upper, ((1,), (1,)))
        second = jnp.where(lane <= sub, second, 0.0)
        full.append(f)
        one.append(fb)
        two.append(second)
        invs.append(eye / jnp.sum(jnp.where(lane == sub, second, 0.0), axis=1, keepdims=True))
    s = 1
    while s < V:
        pick = (lane // (2 * s) == sub // (2 * s)) & (lane // s != sub // s) & (lane < sub)
        t = [dotf(jnp.where(pick, l2, 0.0), x, ((1,), (0,))) for l2, x in zip(two, invs)]
        invs = [x - dotf(x, y, ((1,), (0,))) for x, y in zip(invs, t)]
        s *= 2
    return full, one, invs


def pack(mats, ref):
    lane, sub = square_iotas()
    for p in range(K // 2):
        a, b = mats[2 * p], mats[2 * p + 1]
        both = jnp.where(sub >= lane, a, b).reshape(8, 16, V)
        ref[8 * p : 8 * p + 8, 0:16] = both
        ref[8 * p : 8 * p + 8, 16:17] = jnp.zeros((8, 1, V), F32)
        ref[8 * p, 16:17] = jnp.sum(jnp.where(sub == lane, b, 0.0), axis=0, keepdims=True)


def unpack(ref, scale):
    lane, sub = square_iotas()
    mats = []
    for p in range(K // 2):
        both = ref[8 * p : 8 * p + 8, 0:16].reshape(V, V) * scale
        turned = both.T
        diag = ref[8 * p, 16:17] * scale
        mats.append(jnp.where(sub >= lane, both, turned))
        mats.append(jnp.where(sub == lane, diag, jnp.where(sub < lane, both, turned)))
    return mats


class Summed:
    def __init__(self, refs, place):
        self.x, self.one, self.two, self.out = refs[:4]
        self.sems = refs[4:]
        self.place = place
        self.sent = []

    def copies(self, stage, count, source, target, device):
        send, recv = self.sems[2 * stage], self.sems[2 * stage + 1]
        made = [
            pltpu.make_async_remote_copy(
                src_ref=source(d),
                dst_ref=target(d),
                send_sem=send.at[d],
                recv_sem=recv.at[d],
                device_id=device(d)[1],
                device_id_type=MESH,
            )
            for d in range(1, count)
        ]
        for copy in made:
            copy.start()
        self.sent += made
        self.pending = made

    def arrived(self):
        for copy in self.pending:
            copy.wait_recv()

    def start_one(self):
        pl_ = self.place
        self.copies(0, pl_.plane, lambda d: self.x.at[pl_.in_plane(d)[0]], lambda d: self.one.at[d], pl_.in_plane)

    def start_two(self):
        self.arrived()
        pl_ = self.place
        total = self.x[pl_.me]
        for d in range(1, pl_.plane):
            total = total + self.one[d]
        self.two[pl_.a] = total
        self.copies(1, pl_.na, lambda d: self.two.at[pl_.a], lambda d: self.two.at[pl_.a], pl_.on_line)

    def start_three(self):
        self.arrived()
        pl_ = self.place
        total = self.two[0]
        for q in range(1, pl_.na):
            total = total + self.two[q]
        self.out[pl_.me] = total
        self.copies(2, pl_.plane, lambda d: self.out.at[pl_.me], lambda d: self.out.at[pl_.me], pl_.in_plane)

    def finish(self):
        self.arrived()

    def drain(self):
        for copy in self.sent:
            copy.wait_send()


class Place:
    def __init__(self):
        self.a, self.b, self.c = (lax.axis_index(n) for n in ("gx", "gy", "gz"))
        self.na, self.nb, self.nc = (lax.axis_size(n) for n in ("gx", "gy", "gz"))
        self.plane = self.nb * self.nc
        self.me = self.b * self.nc + self.c

    def in_plane(self, d):
        m = lax.rem(self.me + d, self.plane)
        return m, (self.a, m // self.nc, lax.rem(m, self.nc))

    def on_line(self, d):
        q = lax.rem(self.a + d, self.na)
        return q, (q, self.b, self.c)


def project_kernel(cells, y_hbm, pot_ref, gram_ref, red_ref, f1_ref, f2_ref, applied_hbm,
                   pad, app, zsend, zrecv, zlow, zhigh, potpad, pott, load_sem, store_sem, halo_send, halo_recv, *sums):
    here = Place()
    a, b, c = here.a, here.b, here.c
    na, nb, nc = here.na, here.nb, here.nc
    first, second = Summed(sums[:10], here), Summed(sums[10:], here)

    loads = [
        pltpu.make_async_copy(y_hbm.at[k], pad.at[k, 1 : BX + 1, 1 : BY + 1], load_sem.at[k])
        for k in range(K)
    ]
    for load in loads:
        load.start()

    barrier = pltpu.get_barrier_semaphore()
    for d in range(1, here.plane):
        pl.semaphore_signal(barrier, inc=1, device_id=here.in_plane(d)[1], device_id_type=MESH)
    for d in range(1, na):
        pl.semaphore_signal(barrier, inc=1, device_id=here.on_line(d)[1], device_id_type=MESH)

    @pl.when(a == 0)
    def _():
        pad[:, 0:1] = jnp.zeros((K, 1, BY + 2, BZ, V), BF16)

    @pl.when(a == na - 1)
    def _():
        pad[:, BX + 1 : BX + 2] = jnp.zeros((K, 1, BY + 2, BZ, V), BF16)

    @pl.when(b == 0)
    def _():
        pad[:, :, 0:1] = jnp.zeros((K, BX + 2, 1, BZ, V), BF16)

    @pl.when(b == nb - 1)
    def _():
        pad[:, :, BY + 1 : BY + 2] = jnp.zeros((K, BX + 2, 1, BZ, V), BF16)

    potpad[...] = jnp.zeros((V, V), F32)
    potpad[:, 0:BZ] = pot_ref[...].reshape(V, BZ) + 6.0
    pott[...] = potpad[...].T[0:BZ]

    grams = []
    for k in range(K):
        loads[k].wait()
        rows = pad[k, 1 : BX + 1, 1 : BY + 1].reshape(BX * BY * BZ, V)
        grams.append(lax.dot_general(rows, rows, (((0,), (0,)), ((), ())), preferred_element_type=F32))
    pack(grams, first.x)

    def face(i, _):
        k, x = i // BX, lax.rem(i, BX)
        low = pad[k, x + 1, 1 : BY + 1, 0:16].astype(F32)[:, 0, :]
        high = pad[k, x + 1, 1 : BY + 1, 16:32].astype(F32)[:, 15, :]
        zsend[k, x] = jnp.where(c == 0, high, low).astype(BF16)
        return 0

    lax.fori_loop(0, K * BX, face, 0)

    pl.semaphore_wait(barrier, here.plane + na - 2)

    first.start_one()

    def halo(i, source, target, device):
        return pltpu.make_async_remote_copy(
            src_ref=source, dst_ref=target, send_sem=halo_send.at[i], recv_sem=halo_recv.at[i],
            device_id=device, device_id_type=MESH)

    inner_y, inner_x = slice(1, BY + 1), slice(1, BX + 1)
    z_copy = halo(0, zsend, zrecv, (a, b, 1 - c))
    y_up = halo(1, pad.at[:, inner_x, BY], pad.at[:, inner_x, 0], (a, lax.rem(b + 1, nb), c))
    y_down = halo(2, pad.at[:, inner_x, 1], pad.at[:, inner_x, BY + 1], (a, lax.rem(b + nb - 1, nb), c))
    x_up = halo(3, pad.at[:, BX, inner_y], pad.at[:, 0, inner_y], (lax.rem(a + 1, na), b, c))
    x_down = halo(4, pad.at[:, 1, inner_y], pad.at[:, BX + 1, inner_y], (lax.rem(a + na - 1, na), b, c))
    z_copy.start()
    pl.when(b < nb - 1)(y_up.start)
    pl.when(b > 0)(y_down.start)
    pl.when(a < na - 1)(x_up.start)
    pl.when(a > 0)(x_down.start)

    first.start_two()
    first.start_three()

    z_copy.wait_recv()
    pl.when(b > 0)(y_up.wait_recv)
    pl.when(b < nb - 1)(y_down.wait_recv)

    def spread(i, _):
        k, x = i // BX, lax.rem(i, BX)
        got = zrecv[k, x].astype(F32)
        zhigh[k, x] = jnp.where(c == 0, got, 0.0)
        zlow[k, x] = jnp.where(c == 0, 0.0, got)
        return 0

    lax.fori_loop(0, K * BX, spread, 0)
    zsub = lax.broadcasted_iota(jnp.int32, (BZ, V), 0)

    def plane(x):
        columns = pltpu.roll(pott[...], lax.rem(V - x * BY, V), 1)
        for y in range(BY):
            weight = jnp.broadcast_to(columns[:, y : y + 1], (BZ, V))
            for k in range(K):
                center = pad[k, x + 1, y + 1].astype(F32)
                beside = pad[k, x + 2, y + 1].astype(F32) + pad[k, x, y + 1].astype(F32)
                beside = beside + pad[k, x + 1, y + 2].astype(F32)
                beside = beside + pad[k, x + 1, y].astype(F32)
                up = jnp.where(zsub == BZ - 1, zhigh[k, x, y : y + 1], pltpu.roll(center, BZ - 1, 0))
                down = jnp.where(zsub == 0, zlow[k, x, y : y + 1], pltpu.roll(center, 1, 0))
                app[k, x, y] = (weight * center - (beside + up + down)).astype(BF16)

    def inner(x, _):
        plane(x)
        return 0

    lax.fori_loop(1, BX - 1, inner, 0)
    pl.when(a > 0)(x_up.wait_recv)
    pl.when(a < na - 1)(x_down.wait_recv)
    lax.fori_loop(0, 2, lambda i, _: inner(i * (BX - 1), _), 0)

    stores = [pltpu.make_async_copy(app.at[k], applied_hbm.at[k], store_sem.at[k]) for k in range(K)]
    for store in stores:
        store.start()
    crossed = []
    for k in range(K):
        rows = pad[k, 1 : BX + 1, 1 : BY + 1].reshape(BX * BY * BZ, V)
        image = app[k].reshape(BX * BY * BZ, V)
        part = lax.dot_general(rows, image, (((0,), (0,)), ((), ())), preferred_element_type=F32)
        crossed.append(part + part.T)
    pack(crossed, second.x)
    second.start_one()

    first.finish()
    grams = unpack(first.out, 1.0 / cells)
    for k in range(K):
        gram_ref[k] = grams[k]

    def between(i):
        if i == 1:
            second.start_two()
        if i == 3:
            second.start_three()

    full, one, two = factors(grams, between)
    for k in range(K):
        f1_ref[k] = one[k]
        f2_ref[k] = two[k].astype(BF16)
    second.finish()
    sides = unpack(second.out, 0.5 / cells)
    for k in range(K):
        half = dotf(full[k], sides[k], ((1,), (0,)))
        red_ref[k] = dotf(half, full[k], ((1,), (1,)))

    first.drain()
    second.drain()
    for store in stores:
        store.wait()
    z_copy.wait_send()
    pl.when(b < nb - 1)(y_up.wait_send)
    pl.when(b > 0)(y_down.wait_send)
    pl.when(a < na - 1)(x_up.wait_send)
    pl.when(a > 0)(x_down.wait_send)


def project(subspace, potential, cells):
    na, plane = lax.axis_size("gx"), lax.axis_size("gy") * lax.axis_size("gz")
    dma = pltpu.SemaphoreType.DMA
    vmem = pl.BlockSpec(memory_space=pltpu.VMEM)
    hbm = pl.BlockSpec(memory_space=pl.ANY)
    summed = [pltpu.VMEM((n, CHUNK, V), F32) for n in (plane, plane, na, plane)]
    summed += [dma((n,)) for n in (plane, plane, na, na, plane, plane)]
    square = jax.ShapeDtypeStruct((K, V, V), F32)
    narrow = jax.ShapeDtypeStruct((K, V, V), BF16)
    return pl.pallas_call(
        functools.partial(project_kernel, cells),
        out_shape=(square, square, narrow, narrow, jax.ShapeDtypeStruct(subspace.shape, BF16)),
        in_specs=[hbm, vmem],
        out_specs=(vmem, vmem, vmem, vmem, hbm),
        scratch_shapes=[
            pltpu.VMEM((K, BX + 2, BY + 2, BZ, V), BF16),
            pltpu.VMEM((K, BX, BY, BZ, V), BF16),
            pltpu.VMEM((K, BX, BY, V), BF16),
            pltpu.VMEM((K, BX, BY, V), BF16),
            pltpu.VMEM((K, BX, BY, V), F32),
            pltpu.VMEM((K, BX, BY, V), F32),
            pltpu.VMEM((V, V), F32),
            pltpu.VMEM((BZ, V), F32),
            dma((K,)),
            dma((K,)),
            dma((5,)),
            dma((5,)),
        ]
        + summed
        + summed,
        compiler_params=pltpu.CompilerParams(
            collective_id=0, has_side_effects=True, vmem_limit_bytes=48 << 20
        ),
    )(subspace, potential)


def finish_kernel(y, image, f1, f2, gram, red, y_out, image_out, gram_out, red_out):
    gram_out[...] = gram[...]
    red_out[...] = red[...]
    for source, target in ((y, y_out), (image, image_out)):
        rows = source[0]
        for factor in (f1, f2):
            rows = lax.dot_general(
                rows, factor[0], (((1,), (1,)), ((), ())), preferred_element_type=F32
            ).astype(BF16)
        target[0] = rows


def finish(y, image, f1, f2, gram, red):
    rows = pl.BlockSpec((1, y.shape[1], V), lambda k: (k, 0, 0))
    square = pl.BlockSpec((1, V, V), lambda k: (k, 0, 0))
    small = jax.ShapeDtypeStruct((K, V, V), F32)
    large = jax.ShapeDtypeStruct(y.shape, BF16)
    return pl.pallas_call(
        finish_kernel,
        grid=(K,),
        in_specs=[rows, rows, square, square, square, square],
        out_specs=(rows, rows, square, square),
        out_shape=(large, large, small, small),
        compiler_params=pltpu.CompilerParams(vmem_limit_bytes=40 << 20),
    )(y, image, f1, f2, gram, red)


def per_device(subspace, potential):
    cells = BX * BY * BZ * lax.axis_size("gx") * lax.axis_size("gy") * lax.axis_size("gz")
    gram, red, f1, f2, applied = project(subspace, potential, cells)
    flat = (K, BX * BY * BZ, V)
    basis, image, gram, red = finish(
        subspace.reshape(flat), applied.reshape(flat), f1, f2, gram, red
    )
    return basis.reshape(subspace.shape), image.reshape(subspace.shape), red, gram


def solution(mesh):
    return jax.shard_map(
        per_device,
        mesh=mesh,
        in_specs=(P(None, "gx", "gy", "gz", None), P("gx", "gy", "gz")),
        out_specs=(P(None, "gx", "gy", "gz", None), P(None, "gx", "gy", "gz", None), P(), P()),
        check_vma=False,
    )
```

```python
import functools

import jax
import jax.numpy as jnp
from jax import lax
from jax.experimental import pallas as pl
from jax.experimental.pallas import tpu as pltpu
from jax.sharding import PartitionSpec as P

MESH = pl.DeviceIdType.MESH
HIGHEST = lax.Precision.HIGHEST
BF16 = jnp.bfloat16
F32 = jnp.float32
V = 128
K = 4
BX, BY, BZ = 8, 16, 32
CHUNK = 17
EARLY = 2


def dotf(a, b, dims):
    return lax.dot_general(a, b, (dims, ((), ())), precision=HIGHEST, preferred_element_type=F32)


def square_iotas():
    shape = (V, V)
    return lax.broadcasted_iota(jnp.int32, shape, 1), lax.broadcasted_iota(jnp.int32, shape, 0)


def sub_row(x, j):
    return jnp.broadcast_to(x[j : j + 1, :], (8, V))


def lane_column(x, j):
    return jnp.broadcast_to(x[:, j : j + 1], (8, V))


def eliminate_block(tiles, jb, base, lane, sub):
    rows = range(jb, len(tiles))
    columns = {i: [lane_column(tiles[i], base + q) for q in range(8)] for i in rows}
    for j in range(8):
        inv = 1.0 / sub_row(columns[jb][j], j)
        row = inv * jnp.where(lane == base + j, 1.0, sub_row(tiles[jb], j))
        ahead = {q: sub_row(columns[jb][q], j) * inv for q in range(j + 1, 8)}
        for i in rows:
            if i == jb and j == 7:
                continue
            col = columns[i][j]
            gone = lane == base + j
            if i == jb:
                col = jnp.where(sub > j, col, 0.0)
                gone = gone & (sub > j)
            for q in ahead:
                columns[i][q] = columns[i][q] - col * ahead[q]
            tiles[i] = jnp.where(gone, 0.0, tiles[i]) - col * row


def eliminate(mats, width, after_panel):
    lane = lax.broadcasted_iota(jnp.int32, (width, V), 1)
    sub = lax.broadcasted_iota(jnp.int32, (width, V), 0)
    done = [[] for _ in mats]
    mats = list(mats)
    for start in range(0, V, width):
        stop = start + width
        tiles = [[m[i : i + 8] for i in range(start, stop, 8)] for m in mats]
        for jb in range(width // 8):
            for t in tiles:
                eliminate_block(t, jb, start + 8 * jb, lane[:8], sub[:8])
        panels = [jnp.concatenate(t, axis=0) for t in tiles]
        for rows, p in zip(done, panels):
            rows.append(p)
        if stop < V:
            for k, p in enumerate(panels):
                eye = lane == sub + start
                diag = jnp.sum(jnp.where(eye, p, 0.0), axis=1, keepdims=True)
                left = jnp.where(lane >= stop, p / diag, 0.0)
                upper = (lane > sub + start) & (lane < stop)
                right = jnp.where(upper, 0.0, jnp.where(eye, 1.0, p))
                m = mats[k][stop:]
                ln = lax.broadcasted_iota(jnp.int32, m.shape, 1)
                m = jnp.where((ln >= start) & (ln < stop), 0.0, m)
                update = dotf(left, right, ((0,), (0,)))[stop:]
                mats[k] = jnp.concatenate([mats[k][:stop], m - update], axis=0)
        after_panel(start // width)
    return [jnp.concatenate(rows, axis=0) for rows in done]


def factors(grams, after_panel):
    lane, sub = square_iotas()
    eye = jnp.where(lane == sub, 1.0, 0.0)
    full, one, two = [], [], []
    for m in eliminate(grams, 32, after_panel):
        diag = jnp.sum(jnp.where(lane == sub, m, 0.0), axis=1, keepdims=True)
        scale = lax.rsqrt(diag)
        f = scale * jnp.where(lane < sub, m, eye)
        upper = scale * jnp.where(lane >= sub, m, 0.0)
        fb = f.astype(BF16)
        second = eye + dotf(fb.astype(F32) - f, upper, ((1,), (1,)))
        second = jnp.where(lane <= sub, second, 0.0)
        full.append(f)
        one.append(fb)
        two.append(second)
    after_panel(V)
    powers = []
    same = lane // 16 == sub // 16
    for second in two:
        diag = jnp.sum(jnp.where(lane == sub, second, 0.0), axis=1, keepdims=True)
        powers.append((jnp.where(same & (lane < sub), second, 0.0) / diag, eye / diag))
    start = [p for _, p in powers]
    powers = [p for p, _ in powers]
    invs = [eye - p for p in powers]
    for _ in range(3):
        powers = [dotf(p, p, ((1,), (0,))) for p in powers]
        invs = [x + dotf(x, p, ((1,), (0,))) for x, p in zip(invs, powers)]
    invs = [dotf(x, d, ((1,), (0,))) for x, d in zip(invs, start)]
    s = 16
    while s < V:
        pick = (lane // (2 * s) == sub // (2 * s)) & (lane // s != sub // s) & (lane < sub)
        t = [dotf(jnp.where(pick, l2, 0.0), x, ((1,), (0,))) for l2, x in zip(two, invs)]
        invs = [x - dotf(x, y, ((1,), (0,))) for x, y in zip(invs, t)]
        s *= 2
    return full, one, invs


def pack(mats, ref):
    lane, sub = square_iotas()
    for p in range(K // 2):
        a, b = mats[2 * p], mats[2 * p + 1]
        both = jnp.where(sub >= lane, a, b).reshape(8, 16, V)
        ref[8 * p : 8 * p + 8, 0:16] = both
        ref[8 * p : 8 * p + 8, 16:17] = jnp.zeros((8, 1, V), F32)
        ref[8 * p, 16:17] = jnp.sum(jnp.where(sub == lane, b, 0.0), axis=0, keepdims=True)


def unpack(ref, scale):
    lane, sub = square_iotas()
    mats = []
    for p in range(K // 2):
        both = ref[8 * p : 8 * p + 8, 0:16].reshape(V, V) * scale
        turned = both.T
        diag = ref[8 * p, 16:17] * scale
        mats.append(jnp.where(sub >= lane, both, turned))
        mats.append(jnp.where(sub == lane, diag, jnp.where(sub < lane, both, turned)))
    return mats


class Summed:
    def __init__(self, refs, place):
        self.x, self.one, self.two, self.out = refs[:4]
        self.sems = refs[4:]
        self.place = place
        self.sent = []

    def copies(self, stage, count, source, target, device):
        send, recv = self.sems[2 * stage], self.sems[2 * stage + 1]
        made = [
            pltpu.make_async_remote_copy(
                src_ref=source(d),
                dst_ref=target(d),
                send_sem=send.at[d],
                recv_sem=recv.at[d],
                device_id=device(d)[1],
                device_id_type=MESH,
            )
            for d in range(1, count)
        ]
        for copy in made:
            copy.start()
        self.sent += made
        self.pending = made

    def arrived(self):
        for copy in self.pending:
            copy.wait_recv()

    def start_one(self):
        pl_ = self.place
        self.copies(0, pl_.plane, lambda d: self.x.at[pl_.in_plane(d)[0]], lambda d: self.one.at[d], pl_.in_plane)

    def start_two(self):
        self.arrived()
        pl_ = self.place
        total = self.x[pl_.me]
        for d in range(1, pl_.plane):
            total = total + self.one[d]
        self.two[pl_.a] = total
        self.copies(1, pl_.na, lambda d: self.two.at[pl_.a], lambda d: self.two.at[pl_.a], pl_.on_line)

    def start_three(self):
        self.arrived()
        pl_ = self.place
        total = self.two[0]
        for q in range(1, pl_.na):
            total = total + self.two[q]
        self.out[pl_.me] = total
        self.copies(2, pl_.plane, lambda d: self.out.at[pl_.me], lambda d: self.out.at[pl_.me], pl_.in_plane)

    def finish(self):
        self.arrived()

    def drain(self):
        for copy in self.sent:
            copy.wait_send()


class Place:
    def __init__(self):
        self.a, self.b, self.c = (lax.axis_index(n) for n in ("gx", "gy", "gz"))
        self.na, self.nb, self.nc = (lax.axis_size(n) for n in ("gx", "gy", "gz"))
        self.plane = self.nb * self.nc
        self.me = self.b * self.nc + self.c

    def in_plane(self, d):
        m = lax.rem(self.me + d, self.plane)
        return m, (self.a, m // self.nc, lax.rem(m, self.nc))

    def on_line(self, d):
        q = lax.rem(self.a + d, self.na)
        return q, (q, self.b, self.c)


def project_kernel(cells, y_hbm, pot_hbm, gram_ref, red_ref, f1_ref, f2_ref, applied_hbm,
                   pad, app, zsend, zrecv, zlow, zhigh, potbuf, potpad, pott, load_sem, store_sem, halo_send, halo_recv, *sums):
    here = Place()
    a, b, c = here.a, here.b, here.c
    na, nb, nc = here.na, here.nb, here.nc
    first, second = Summed(sums[:10], here), Summed(sums[10:], here)

    loads = [
        pltpu.make_async_copy(y_hbm.at[k], pad.at[k, 1 : BX + 1, 1 : BY + 1], load_sem.at[k])
        for k in range(K)
    ]
    loads.append(pltpu.make_async_copy(pot_hbm, potbuf, load_sem.at[K]))
    for load in loads:
        load.start()

    barrier = pltpu.get_barrier_semaphore()
    for d in range(1, here.plane):
        pl.semaphore_signal(barrier, inc=1, device_id=here.in_plane(d)[1], device_id_type=MESH)
    for d in range(1, na):
        pl.semaphore_signal(barrier, inc=1, device_id=here.on_line(d)[1], device_id_type=MESH)

    @pl.when(a == 0)
    def _():
        pad[:, 0:1] = jnp.zeros((K, 1, BY + 2, BZ, V), BF16)

    @pl.when(a == na - 1)
    def _():
        pad[:, BX + 1 : BX + 2] = jnp.zeros((K, 1, BY + 2, BZ, V), BF16)

    @pl.when(b == 0)
    def _():
        pad[:, :, 0:1] = jnp.zeros((K, BX + 2, 1, BZ, V), BF16)

    @pl.when(b == nb - 1)
    def _():
        pad[:, :, BY + 1 : BY + 2] = jnp.zeros((K, BX + 2, 1, BZ, V), BF16)

    loads[K].wait()
    potpad[...] = jnp.zeros((V, V), F32)
    potpad[:, 0:BZ] = potbuf[...].reshape(V, BZ) + 6.0
    pott[...] = potpad[...].T[0:BZ]

    grams = []
    for k in range(K):
        loads[k].wait()
        rows = pad[k, 1 : BX + 1, 1 : BY + 1].reshape(BX * BY * BZ, V)
        grams.append(lax.dot_general(rows, rows, (((0,), (0,)), ((), ())), preferred_element_type=F32))
    pack(grams, first.x)

    def face(i, _):
        k, x = i // BX, lax.rem(i, BX)
        low = pad[k, x + 1, 1 : BY + 1, 0:16].astype(F32)[:, 0, :]
        high = pad[k, x + 1, 1 : BY + 1, 16:32].astype(F32)[:, 15, :]
        zsend[k, x] = jnp.where(c == 0, high, low).astype(BF16)
        return 0

    lax.fori_loop(0, K * BX, face, 0)

    pl.semaphore_wait(barrier, here.plane + na - 2)

    first.start_one()

    def halo(i, source, target, device):
        return [
            pltpu.make_async_remote_copy(
                src_ref=source(k),
                dst_ref=target(k),
                send_sem=halo_send.at[i, k],
                recv_sem=halo_recv.at[i, k],
                device_id=device,
                device_id_type=MESH,
            )
            for k in range(K)
        ]

    inner_y, inner_x = slice(1, BY + 1), slice(1, BX + 1)
    z_copy = halo(0, lambda k: zsend.at[k], lambda k: zrecv.at[k], (a, b, 1 - c))
    y_up = halo(
        1, lambda k: pad.at[k, inner_x, BY], lambda k: pad.at[k, inner_x, 0], (a, lax.rem(b + 1, nb), c)
    )
    y_down = halo(
        2, lambda k: pad.at[k, inner_x, 1], lambda k: pad.at[k, inner_x, BY + 1], (a, lax.rem(b + nb - 1, nb), c)
    )
    x_up = halo(
        3, lambda k: pad.at[k, BX, inner_y], lambda k: pad.at[k, 0, inner_y], (lax.rem(a + 1, na), b, c)
    )
    x_down = halo(
        4, lambda k: pad.at[k, 1, inner_y], lambda k: pad.at[k, BX + 1, inner_y], (lax.rem(a + na - 1, na), b, c)
    )

    def each(copies, what):
        def act():
            for copy in copies:
                getattr(copy, what)()

        return act

    each(z_copy, "start")()
    pl.when(b < nb - 1)(each(y_up, "start"))
    pl.when(b > 0)(each(y_down, "start"))

    each(z_copy, "wait_recv")()

    def spread(i, _):
        k, x = i // BX, lax.rem(i, BX)
        got = zrecv[k, x].astype(F32)
        zhigh[k, x] = jnp.where(c == 0, got, 0.0)
        zlow[k, x] = jnp.where(c == 0, 0.0, got)
        return 0

    lax.fori_loop(0, K * BX, spread, 0)
    zsub = lax.broadcasted_iota(jnp.int32, (BZ, V), 0)

    def cells_of(x, ys):
        columns = pltpu.roll(pott[...], lax.rem(V - x * BY, V), 1)
        for y in ys:
            weight = jnp.broadcast_to(columns[:, y : y + 1], (BZ, V))
            for k in range(K):
                center = pad[k, x + 1, y + 1].astype(F32)
                beside = pad[k, x + 2, y + 1].astype(F32) + pad[k, x, y + 1].astype(F32)
                beside = beside + pad[k, x + 1, y + 2].astype(F32)
                beside = beside + pad[k, x + 1, y].astype(F32)
                up = jnp.where(zsub == BZ - 1, zhigh[k, x, y : y + 1], pltpu.roll(center, BZ - 1, 0))
                down = jnp.where(zsub == 0, zlow[k, x, y : y + 1], pltpu.roll(center, 1, 0))
                app[k, x, y] = (weight * center - (beside + up + down)).astype(BF16)

    def planes(first_x, count, step, ys):
        def body(i, _):
            cells_of(first_x + i * step, ys)
            return 0

        lax.fori_loop(0, count, body, 0)

    planes(1, EARLY, 1, range(1, BY - 1))
    first.start_two()
    pl.when(a < na - 1)(each(x_up, "start"))
    pl.when(a > 0)(each(x_down, "start"))
    planes(1 + EARLY, BX - 2 - EARLY, 1, range(1, BY - 1))
    first.start_three()
    pl.when(b > 0)(each(y_up, "wait_recv"))
    pl.when(b < nb - 1)(each(y_down, "wait_recv"))
    planes(1, BX - 2, 1, (0, BY - 1))
    pl.when(a > 0)(each(x_up, "wait_recv"))
    pl.when(a < na - 1)(each(x_down, "wait_recv"))
    planes(0, 2, BX - 1, range(BY))

    stores = [pltpu.make_async_copy(app.at[k], applied_hbm.at[k], store_sem.at[k]) for k in range(K)]
    for store in stores:
        store.start()
    crossed = []
    for k in range(K):
        rows = pad[k, 1 : BX + 1, 1 : BY + 1].reshape(BX * BY * BZ, V)
        image = app[k].reshape(BX * BY * BZ, V)
        part = lax.dot_general(rows, image, (((0,), (0,)), ((), ())), preferred_element_type=F32)
        crossed.append(part + part.T)
    pack(crossed, second.x)
    second.start_one()

    first.finish()
    grams = unpack(first.out, 1.0 / cells)
    for k in range(K):
        gram_ref[k] = grams[k]

    def between(i):
        if i == 3:
            second.start_two()

    full, one, two = factors(grams, between)
    for k in range(K):
        f1_ref[k] = one[k]
        f2_ref[k] = two[k].astype(BF16)
    second.start_three()
    second.finish()
    sides = unpack(second.out, 0.5 / cells)
    for k in range(K):
        half = dotf(full[k], sides[k], ((1,), (0,)))
        red_ref[k] = dotf(half, full[k], ((1,), (1,)))

    first.drain()
    second.drain()
    for store in stores:
        store.wait()
    each(z_copy, "wait_send")()
    pl.when(a < na - 1)(each(x_up, "wait_send"))
    pl.when(b < nb - 1)(each(y_up, "wait_send"))
    pl.when(a > 0)(each(x_down, "wait_send"))
    pl.when(b > 0)(each(y_down, "wait_send"))


def project(subspace, potential, cells):
    na, plane = lax.axis_size("gx"), lax.axis_size("gy") * lax.axis_size("gz")
    dma = pltpu.SemaphoreType.DMA
    vmem = pl.BlockSpec(memory_space=pltpu.VMEM)
    hbm = pl.BlockSpec(memory_space=pl.ANY)
    summed = [pltpu.VMEM((n, CHUNK, V), F32) for n in (plane, plane, na, plane)]
    summed += [dma((n,)) for n in (plane, plane, na, na, plane, plane)]
    square = jax.ShapeDtypeStruct((K, V, V), F32)
    narrow = jax.ShapeDtypeStruct((K, V, V), BF16)
    return pl.pallas_call(
        functools.partial(project_kernel, cells),
        out_shape=(square, square, narrow, narrow, jax.ShapeDtypeStruct(subspace.shape, BF16)),
        in_specs=[hbm, hbm],
        out_specs=(vmem, vmem, vmem, vmem, hbm),
        scratch_shapes=[
            pltpu.VMEM((K, BX + 2, BY + 2, BZ, V), BF16),
            pltpu.VMEM((K, BX, BY, BZ, V), BF16),
            pltpu.VMEM((K, BX, BY, V), BF16),
            pltpu.VMEM((K, BX, BY, V), BF16),
            pltpu.VMEM((K, BX, BY, V), F32),
            pltpu.VMEM((K, BX, BY, V), F32),
            pltpu.VMEM((BX, BY, BZ), F32),
            pltpu.VMEM((V, V), F32),
            pltpu.VMEM((BZ, V), F32),
            dma((K + 1,)),
            dma((K,)),
            dma((5, K)),
            dma((5, K)),
        ]
        + summed
        + summed,
        compiler_params=pltpu.CompilerParams(
            collective_id=0, has_side_effects=True, vmem_limit_bytes=48 << 20
        ),
    )(subspace, potential)


def finish_kernel(y, image, f1, f2, gram, red, y_out, image_out, gram_out, red_out):
    gram_out[...] = gram[...]
    red_out[...] = red[...]
    for source, target in ((y, y_out), (image, image_out)):
        rows = source[0]
        for factor in (f1, f2):
            rows = lax.dot_general(
                rows, factor[0], (((1,), (1,)), ((), ())), preferred_element_type=F32
            ).astype(BF16)
        target[0] = rows


def finish(y, image, f1, f2, gram, red):
    rows = pl.BlockSpec((1, y.shape[1], V), lambda k: (k, 0, 0))
    square = pl.BlockSpec((1, V, V), lambda k: (k, 0, 0))
    small = jax.ShapeDtypeStruct((K, V, V), F32)
    large = jax.ShapeDtypeStruct(y.shape, BF16)
    return pl.pallas_call(
        finish_kernel,
        grid=(K,),
        in_specs=[rows, rows, square, square, square, square],
        out_specs=(rows, rows, square, square),
        out_shape=(large, large, small, small),
        compiler_params=pltpu.CompilerParams(vmem_limit_bytes=40 << 20),
    )(y, image, f1, f2, gram, red)


def per_device(subspace, potential):
    cells = BX * BY * BZ * lax.axis_size("gx") * lax.axis_size("gy") * lax.axis_size("gz")
    gram, red, f1, f2, applied = project(subspace, potential, cells)
    flat = (K, BX * BY * BZ, V)
    basis, image, gram, red = finish(
        subspace.reshape(flat), applied.reshape(flat), f1, f2, gram, red
    )
    return basis.reshape(subspace.shape), image.reshape(subspace.shape), red, gram


def solution(mesh):
    return jax.shard_map(
        per_device,
        mesh=mesh,
        in_specs=(P(None, "gx", "gy", "gz", None), P("gx", "gy", "gz")),
        out_specs=(P(None, "gx", "gy", "gz", None), P(None, "gx", "gy", "gz", None), P(), P()),
        check_vma=False,
    )
```

```python
import functools

import jax
import jax.numpy as jnp
from jax import lax
from jax.experimental import pallas as pl
from jax.experimental.pallas import tpu as pltpu
from jax.sharding import PartitionSpec as P

MESH = pl.DeviceIdType.MESH
HIGHEST = lax.Precision.HIGHEST
BF16 = jnp.bfloat16
F32 = jnp.float32
V = 128
K = 4
BX, BY, BZ = 8, 16, 32
CHUNK = 17
EARLY = 2


def dotf(a, b, dims):
    return lax.dot_general(a, b, (dims, ((), ())), precision=HIGHEST, preferred_element_type=F32)


def square_iotas():
    shape = (V, V)
    return lax.broadcasted_iota(jnp.int32, shape, 1), lax.broadcasted_iota(jnp.int32, shape, 0)


def sub_row(x, j):
    return jnp.broadcast_to(x[j : j + 1, :], (8, V))


def lane_column(x, j):
    return jnp.broadcast_to(x[:, j : j + 1], (8, V))


def eliminate_block(tiles, jb, base, lane, sub):
    rows = range(jb, len(tiles))
    columns = {i: [lane_column(tiles[i], base + q) for q in range(8)] for i in rows}
    for j in range(8):
        inv = 1.0 / sub_row(columns[jb][j], j)
        row = inv * jnp.where(lane == base + j, 1.0, sub_row(tiles[jb], j))
        ahead = {q: sub_row(columns[jb][q], j) * inv for q in range(j + 1, 8)}
        for i in rows:
            if i == jb and j == 7:
                continue
            col = columns[i][j]
            gone = lane == base + j
            if i == jb:
                col = jnp.where(sub > j, col, 0.0)
                gone = gone & (sub > j)
            for q in ahead:
                columns[i][q] = columns[i][q] - col * ahead[q]
            tiles[i] = jnp.where(gone, 0.0, tiles[i]) - col * row


def eliminate(mats, width, after_panel):
    lane = lax.broadcasted_iota(jnp.int32, (width, V), 1)
    sub = lax.broadcasted_iota(jnp.int32, (width, V), 0)
    done = [[] for _ in mats]
    mats = list(mats)
    for start in range(0, V, width):
        stop = start + width
        tiles = [[m[i : i + 8] for i in range(start, stop, 8)] for m in mats]
        for jb in range(width // 8):
            for t in tiles:
                eliminate_block(t, jb, start + 8 * jb, lane[:8], sub[:8])
        panels = [jnp.concatenate(t, axis=0) for t in tiles]
        for rows, p in zip(done, panels):
            rows.append(p)
        if stop < V:
            for k, p in enumerate(panels):
                eye = lane == sub + start
                diag = jnp.sum(jnp.where(eye, p, 0.0), axis=1, keepdims=True)
                left = jnp.where(lane >= stop, p / diag, 0.0)
                upper = (lane > sub + start) & (lane < stop)
                right = jnp.where(upper, 0.0, jnp.where(eye, 1.0, p))
                m = mats[k][stop:]
                ln = lax.broadcasted_iota(jnp.int32, m.shape, 1)
                m = jnp.where((ln >= start) & (ln < stop), 0.0, m)
                update = dotf(left, right, ((0,), (0,)))[stop:]
                mats[k] = jnp.concatenate([mats[k][:stop], m - update], axis=0)
        after_panel(start // width)
    return [jnp.concatenate(rows, axis=0) for rows in done]


def factors(grams, after_panel):
    lane, sub = square_iotas()
    eye = jnp.where(lane == sub, 1.0, 0.0)
    full, one, two = [], [], []
    for m in eliminate(grams, 32, after_panel):
        diag = jnp.sum(jnp.where(lane == sub, m, 0.0), axis=1, keepdims=True)
        scale = lax.rsqrt(diag)
        f = scale * jnp.where(lane < sub, m, eye)
        upper = scale * jnp.where(lane >= sub, m, 0.0)
        fb = f.astype(BF16)
        second = eye + dotf(fb.astype(F32) - f, upper, ((1,), (1,)))
        second = jnp.where(lane <= sub, second, 0.0)
        full.append(f)
        one.append(fb)
        two.append(second)
    after_panel(V)
    powers = []
    same = lane // 16 == sub // 16
    for second in two:
        diag = jnp.sum(jnp.where(lane == sub, second, 0.0), axis=1, keepdims=True)
        powers.append((jnp.where(same & (lane < sub), second, 0.0) / diag, eye / diag))
    start = [p for _, p in powers]
    powers = [p for p, _ in powers]
    invs = [eye - p for p in powers]
    for _ in range(3):
        powers = [dotf(p, p, ((1,), (0,))) for p in powers]
        invs = [x + dotf(x, p, ((1,), (0,))) for x, p in zip(invs, powers)]
    invs = [dotf(x, d, ((1,), (0,))) for x, d in zip(invs, start)]
    s = 16
    while s < V:
        pick = (lane // (2 * s) == sub // (2 * s)) & (lane // s != sub // s) & (lane < sub)
        t = [dotf(jnp.where(pick, l2, 0.0), x, ((1,), (0,))) for l2, x in zip(two, invs)]
        invs = [x - dotf(x, y, ((1,), (0,))) for x, y in zip(invs, t)]
        s *= 2
    return full, one, invs


def pack(mats, ref):
    lane, sub = square_iotas()
    for p in range(K // 2):
        a, b = mats[2 * p], mats[2 * p + 1]
        both = jnp.where(sub >= lane, a, b).reshape(8, 16, V)
        ref[8 * p : 8 * p + 8, 0:16] = both
        ref[8 * p : 8 * p + 8, 16:17] = jnp.zeros((8, 1, V), F32)
        ref[8 * p, 16:17] = jnp.sum(jnp.where(sub == lane, b, 0.0), axis=0, keepdims=True)


def unpack(ref, scale):
    lane, sub = square_iotas()
    mats = []
    for p in range(K // 2):
        both = ref[8 * p : 8 * p + 8, 0:16].reshape(V, V) * scale
        turned = both.T
        diag = ref[8 * p, 16:17] * scale
        mats.append(jnp.where(sub >= lane, both, turned))
        mats.append(jnp.where(sub == lane, diag, jnp.where(sub < lane, both, turned)))
    return mats


class Summed:
    def __init__(self, refs, place):
        self.x, self.one, self.two, self.out = refs[:4]
        self.sems = refs[4:]
        self.place = place
        self.sent = []

    def copies(self, stage, count, source, target, device):
        send, recv = self.sems[2 * stage], self.sems[2 * stage + 1]
        made = [
            pltpu.make_async_remote_copy(
                src_ref=source(d),
                dst_ref=target(d),
                send_sem=send.at[d],
                recv_sem=recv.at[d],
                device_id=device(d)[1],
                device_id_type=MESH,
            )
            for d in range(1, count)
        ]
        for copy in made:
            copy.start()
        self.sent += made
        self.pending = made

    def arrived(self):
        for copy in self.pending:
            copy.wait_recv()

    def start_one(self):
        pl_ = self.place
        self.copies(0, pl_.plane, lambda d: self.x.at[pl_.in_plane(d)[0]], lambda d: self.one.at[d], pl_.in_plane)

    def start_two(self):
        self.arrived()
        pl_ = self.place
        total = self.x[pl_.me]
        for d in range(1, pl_.plane):
            total = total + self.one[d]
        self.two[pl_.a] = total
        self.copies(1, pl_.na, lambda d: self.two.at[pl_.a], lambda d: self.two.at[pl_.a], pl_.on_line)

    def start_three(self):
        self.arrived()
        pl_ = self.place
        total = self.two[0]
        for q in range(1, pl_.na):
            total = total + self.two[q]
        self.out[pl_.me] = total
        self.copies(2, pl_.plane, lambda d: self.out.at[pl_.me], lambda d: self.out.at[pl_.me], pl_.in_plane)

    def finish(self):
        self.arrived()

    def drain(self):
        for copy in self.sent:
            copy.wait_send()


class Place:
    def __init__(self):
        self.a, self.b, self.c = (lax.axis_index(n) for n in ("gx", "gy", "gz"))
        self.na, self.nb, self.nc = (lax.axis_size(n) for n in ("gx", "gy", "gz"))
        self.plane = self.nb * self.nc
        self.me = self.b * self.nc + self.c

    def in_plane(self, d):
        m = lax.rem(self.me + d, self.plane)
        return m, (self.a, m // self.nc, lax.rem(m, self.nc))

    def on_line(self, d):
        q = lax.rem(self.a + d, self.na)
        return q, (q, self.b, self.c)


def apply(rows, factor):
    return lax.dot_general(
        rows, factor, (((1,), (1,)), ((), ())), preferred_element_type=F32
    ).astype(BF16)


def project_kernel(cells, y_hbm, pot_hbm, gram_ref, red_ref, f2_ref, basis_hbm, image_hbm,
                   pad, app, base, zsend, zrecv, zlow, zhigh, potbuf, potpad, pott, load_sem, store_sem, halo_send, halo_recv, *sums):
    here = Place()
    a, b, c = here.a, here.b, here.c
    na, nb, nc = here.na, here.nb, here.nc
    first, second = Summed(sums[:10], here), Summed(sums[10:], here)

    loads = [
        pltpu.make_async_copy(y_hbm.at[k], pad.at[k, 1 : BX + 1, 1 : BY + 1], load_sem.at[k])
        for k in range(K)
    ]
    loads.append(pltpu.make_async_copy(pot_hbm, potbuf, load_sem.at[K]))
    for load in loads:
        load.start()

    barrier = pltpu.get_barrier_semaphore()
    for d in range(1, here.plane):
        pl.semaphore_signal(barrier, inc=1, device_id=here.in_plane(d)[1], device_id_type=MESH)
    for d in range(1, na):
        pl.semaphore_signal(barrier, inc=1, device_id=here.on_line(d)[1], device_id_type=MESH)

    @pl.when(a == 0)
    def _():
        pad[:, 0:1] = jnp.zeros((K, 1, BY + 2, BZ, V), BF16)

    @pl.when(a == na - 1)
    def _():
        pad[:, BX + 1 : BX + 2] = jnp.zeros((K, 1, BY + 2, BZ, V), BF16)

    @pl.when(b == 0)
    def _():
        pad[:, :, 0:1] = jnp.zeros((K, BX + 2, 1, BZ, V), BF16)

    @pl.when(b == nb - 1)
    def _():
        pad[:, :, BY + 1 : BY + 2] = jnp.zeros((K, BX + 2, 1, BZ, V), BF16)

    loads[K].wait()
    potpad[...] = jnp.zeros((V, V), F32)
    potpad[:, 0:BZ] = potbuf[...].reshape(V, BZ) + 6.0
    pott[...] = potpad[...].T[0:BZ]

    grams = []
    for k in range(K):
        loads[k].wait()
        rows = pad[k, 1 : BX + 1, 1 : BY + 1].reshape(BX * BY * BZ, V)
        grams.append(lax.dot_general(rows, rows, (((0,), (0,)), ((), ())), preferred_element_type=F32))
    pack(grams, first.x)

    def face(i, _):
        k, x = i // BX, lax.rem(i, BX)
        low = pad[k, x + 1, 1 : BY + 1, 0:16].astype(F32)[:, 0, :]
        high = pad[k, x + 1, 1 : BY + 1, 16:32].astype(F32)[:, 15, :]
        zsend[k, x] = jnp.where(c == 0, high, low).astype(BF16)
        return 0

    lax.fori_loop(0, K * BX, face, 0)

    pl.semaphore_wait(barrier, here.plane + na - 2)

    first.start_one()

    def halo(i, source, target, device):
        return [
            pltpu.make_async_remote_copy(
                src_ref=source(k),
                dst_ref=target(k),
                send_sem=halo_send.at[i, k],
                recv_sem=halo_recv.at[i, k],
                device_id=device,
                device_id_type=MESH,
            )
            for k in range(K)
        ]

    inner_y, inner_x = slice(1, BY + 1), slice(1, BX + 1)
    z_copy = halo(0, lambda k: zsend.at[k], lambda k: zrecv.at[k], (a, b, 1 - c))
    y_up = halo(
        1, lambda k: pad.at[k, inner_x, BY], lambda k: pad.at[k, inner_x, 0], (a, lax.rem(b + 1, nb), c)
    )
    y_down = halo(
        2, lambda k: pad.at[k, inner_x, 1], lambda k: pad.at[k, inner_x, BY + 1], (a, lax.rem(b + nb - 1, nb), c)
    )
    x_up = halo(
        3, lambda k: pad.at[k, BX, inner_y], lambda k: pad.at[k, 0, inner_y], (lax.rem(a + 1, na), b, c)
    )
    x_down = halo(
        4, lambda k: pad.at[k, 1, inner_y], lambda k: pad.at[k, BX + 1, inner_y], (lax.rem(a + na - 1, na), b, c)
    )

    def each(copies, what):
        def act():
            for copy in copies:
                getattr(copy, what)()

        return act

    each(z_copy, "start")()
    pl.when(a < na - 1)(each(x_up, "start"))
    pl.when(a > 0)(each(x_down, "start"))

    each(z_copy, "wait_recv")()

    def spread(i, _):
        k, x = i // BX, lax.rem(i, BX)
        got = zrecv[k, x].astype(F32)
        zhigh[k, x] = jnp.where(c == 0, got, 0.0)
        zlow[k, x] = jnp.where(c == 0, 0.0, got)
        return 0

    lax.fori_loop(0, K * BX, spread, 0)
    zsub = lax.broadcasted_iota(jnp.int32, (BZ, V), 0)

    def cells_of(x, ys):
        columns = pltpu.roll(pott[...], lax.rem(V - x * BY, V), 1)
        for y in ys:
            weight = jnp.broadcast_to(columns[:, y : y + 1], (BZ, V))
            for k in range(K):
                center = pad[k, x + 1, y + 1].astype(F32)
                beside = pad[k, x + 2, y + 1].astype(F32) + pad[k, x, y + 1].astype(F32)
                beside = beside + pad[k, x + 1, y + 2].astype(F32)
                beside = beside + pad[k, x + 1, y].astype(F32)
                up = jnp.where(zsub == BZ - 1, zhigh[k, x, y : y + 1], pltpu.roll(center, BZ - 1, 0))
                down = jnp.where(zsub == 0, zlow[k, x, y : y + 1], pltpu.roll(center, 1, 0))
                app[k, x, y] = (weight * center - (beside + up + down)).astype(BF16)

    def planes(first_x, count, step, ys):
        def body(i, _):
            cells_of(first_x + i * step, ys)
            return 0

        lax.fori_loop(0, count, body, 0)

    planes(1, EARLY, 1, range(1, BY - 1))
    first.start_two()
    pl.when(b < nb - 1)(each(y_up, "start"))
    pl.when(b > 0)(each(y_down, "start"))
    planes(1 + EARLY, BX - 2 - EARLY, 1, range(1, BY - 1))
    first.start_three()
    pl.when(b > 0)(each(y_up, "wait_recv"))
    pl.when(b < nb - 1)(each(y_down, "wait_recv"))
    planes(1, BX - 2, 1, (0, BY - 1))
    pl.when(a > 0)(each(x_up, "wait_recv"))
    pl.when(a < na - 1)(each(x_down, "wait_recv"))
    planes(0, 2, BX - 1, range(BY))

    crossed = []
    for k in range(K):
        rows = pad[k, 1 : BX + 1, 1 : BY + 1].reshape(BX * BY * BZ, V)
        image = app[k].reshape(BX * BY * BZ, V)
        part = lax.dot_general(rows, image, (((0,), (0,)), ((), ())), preferred_element_type=F32)
        crossed.append(part + part.T)
    pack(crossed, second.x)
    second.start_one()

    first.finish()
    grams = unpack(first.out, 1.0 / cells)
    for k in range(K):
        gram_ref[k] = grams[k]

    def between(i):
        if i == 2:
            second.start_two()

    full, one, two = factors(grams, between)
    for k in range(K):
        f2_ref[k] = two[k].astype(BF16)
    second.start_three()
    stores = []
    for k in range(K):
        rows = pad[k, 1 : BX + 1, 1 : BY + 1].reshape(BX * BY * BZ, V)
        base[k] = apply(rows, one[k]).reshape(BX, BY, BZ, V)
        rows = app[k].reshape(BX * BY * BZ, V)
        app[k] = apply(rows, one[k]).reshape(BX, BY, BZ, V)
        for i, (source, target) in enumerate(((base, basis_hbm), (app, image_hbm))):
            stores.append(pltpu.make_async_copy(source.at[k], target.at[k], store_sem.at[i, k]))
            stores[-1].start()
    second.finish()
    sides = unpack(second.out, 0.5 / cells)
    for k in range(K):
        half = dotf(full[k], sides[k], ((1,), (0,)))
        red_ref[k] = dotf(half, full[k], ((1,), (1,)))

    first.drain()
    second.drain()
    for store in stores:
        store.wait()
    each(z_copy, "wait_send")()
    pl.when(a < na - 1)(each(x_up, "wait_send"))
    pl.when(b < nb - 1)(each(y_up, "wait_send"))
    pl.when(a > 0)(each(x_down, "wait_send"))
    pl.when(b > 0)(each(y_down, "wait_send"))


def project(subspace, potential, cells):
    na, plane = lax.axis_size("gx"), lax.axis_size("gy") * lax.axis_size("gz")
    dma = pltpu.SemaphoreType.DMA
    vmem = pl.BlockSpec(memory_space=pltpu.VMEM)
    hbm = pl.BlockSpec(memory_space=pl.ANY)
    summed = [pltpu.VMEM((n, CHUNK, V), F32) for n in (plane, plane, na, plane)]
    summed += [dma((n,)) for n in (plane, plane, na, na, plane, plane)]
    square = jax.ShapeDtypeStruct((K, V, V), F32)
    narrow = jax.ShapeDtypeStruct((K, V, V), BF16)
    large = jax.ShapeDtypeStruct(subspace.shape, BF16)
    return pl.pallas_call(
        functools.partial(project_kernel, cells),
        out_shape=(square, square, narrow, large, large),
        in_specs=[hbm, pl.BlockSpec(memory_space=pltpu.HBM)],
        out_specs=(vmem, vmem, vmem, hbm, hbm),
        scratch_shapes=[
            pltpu.VMEM((K, BX + 2, BY + 2, BZ, V), BF16),
            pltpu.VMEM((K, BX, BY, BZ, V), BF16),
            pltpu.VMEM((K, BX, BY, BZ, V), BF16),
            pltpu.VMEM((K, BX, BY, V), BF16),
            pltpu.VMEM((K, BX, BY, V), BF16),
            pltpu.VMEM((K, BX, BY, V), F32),
            pltpu.VMEM((K, BX, BY, V), F32),
            pltpu.VMEM((BX, BY, BZ), F32),
            pltpu.VMEM((V, V), F32),
            pltpu.VMEM((BZ, V), F32),
            dma((K + 1,)),
            dma((2, K)),
            dma((5, K)),
            dma((5, K)),
        ]
        + summed
        + summed,
        compiler_params=pltpu.CompilerParams(
            collective_id=0, has_side_effects=True, vmem_limit_bytes=44 << 20
        ),
    )(subspace, potential)


def finish_kernel(y, image, f2, gram, red, y_out, image_out, gram_out, red_out):
    gram_out[...] = gram[...]
    red_out[...] = red[...]
    y_out[0] = apply(y[0], f2[0])
    image_out[0] = apply(image[0], f2[0])


def finish(y, image, f2, gram, red):
    rows = pl.BlockSpec((1, y.shape[1], V), lambda k: (k, 0, 0))
    square = pl.BlockSpec((1, V, V), lambda k: (k, 0, 0))
    small = jax.ShapeDtypeStruct((K, V, V), F32)
    large = jax.ShapeDtypeStruct(y.shape, BF16)
    return pl.pallas_call(
        finish_kernel,
        grid=(K,),
        in_specs=[rows, rows, square, square, square],
        out_specs=(rows, rows, square, square),
        out_shape=(large, large, small, small),
        compiler_params=pltpu.CompilerParams(vmem_limit_bytes=40 << 20),
    )(y, image, f2, gram, red)


def per_device(subspace, potential):
    cells = BX * BY * BZ * lax.axis_size("gx") * lax.axis_size("gy") * lax.axis_size("gz")
    gram, red, f2, basis, image = project(subspace, potential, cells)
    flat = (K, BX * BY * BZ, V)
    basis, image, gram, red = finish(
        basis.reshape(flat), image.reshape(flat), f2, gram, red
    )
    return basis.reshape(subspace.shape), image.reshape(subspace.shape), red, gram


def solution(mesh):
    return jax.shard_map(
        per_device,
        mesh=mesh,
        in_specs=(P(None, "gx", "gy", "gz", None), P("gx", "gy", "gz")),
        out_specs=(P(None, "gx", "gy", "gz", None), P(None, "gx", "gy", "gz", None), P(), P()),
        check_vma=False,
    )
```

```python
import functools

import jax
import jax.numpy as jnp
from jax import lax
from jax.experimental import pallas as pl
from jax.experimental.pallas import tpu as pltpu
from jax.sharding import PartitionSpec as P

MESH = pl.DeviceIdType.MESH
HIGHEST = lax.Precision.HIGHEST
BF16 = jnp.bfloat16
F32 = jnp.float32
V = 128
K = 4
BX, BY, BZ = 8, 16, 32
CHUNK = 17
EARLY = 2


def dotf(a, b, dims):
    return lax.dot_general(a, b, (dims, ((), ())), precision=HIGHEST, preferred_element_type=F32)


def square_iotas():
    shape = (V, V)
    return lax.broadcasted_iota(jnp.int32, shape, 1), lax.broadcasted_iota(jnp.int32, shape, 0)


def sub_row(x, j):
    return jnp.broadcast_to(x[j : j + 1, :], (8, V))


def lane_column(x, j):
    return jnp.broadcast_to(x[:, j : j + 1], (8, V))


def eliminate_block(tiles, jb, base, lane, sub):
    rows = range(jb, len(tiles))
    columns = {i: [lane_column(tiles[i], base + q) for q in range(8)] for i in rows}
    for j in range(8):
        inv = 1.0 / sub_row(columns[jb][j], j)
        row = inv * jnp.where(lane == base + j, 1.0, sub_row(tiles[jb], j))
        ahead = {q: sub_row(columns[jb][q], j) * inv for q in range(j + 1, 8)}
        for i in rows:
            if i == jb and j == 7:
                continue
            col = columns[i][j]
            gone = lane == base + j
            if i == jb:
                col = jnp.where(sub > j, col, 0.0)
                gone = gone & (sub > j)
            for q in ahead:
                columns[i][q] = columns[i][q] - col * ahead[q]
            tiles[i] = jnp.where(gone, 0.0, tiles[i]) - col * row


def eliminate(mats, width, after_panel):
    lane = lax.broadcasted_iota(jnp.int32, (width, V), 1)
    sub = lax.broadcasted_iota(jnp.int32, (width, V), 0)
    done = [[] for _ in mats]
    mats = list(mats)
    for start in range(0, V, width):
        stop = start + width
        tiles = [[m[i : i + 8] for i in range(start, stop, 8)] for m in mats]
        for jb in range(width // 8):
            for t in tiles:
                eliminate_block(t, jb, start + 8 * jb, lane[:8], sub[:8])
        panels = [jnp.concatenate(t, axis=0) for t in tiles]
        for rows, p in zip(done, panels):
            rows.append(p)
        if stop < V:
            for k, p in enumerate(panels):
                eye = lane == sub + start
                diag = jnp.sum(jnp.where(eye, p, 0.0), axis=1, keepdims=True)
                left = jnp.where(lane >= stop, p / diag, 0.0)
                upper = (lane > sub + start) & (lane < stop)
                right = jnp.where(upper, 0.0, jnp.where(eye, 1.0, p))
                m = mats[k][stop:]
                ln = lax.broadcasted_iota(jnp.int32, m.shape, 1)
                m = jnp.where((ln >= start) & (ln < stop), 0.0, m)
                update = dotf(left, right, ((0,), (0,)))[stop:]
                mats[k] = jnp.concatenate([mats[k][:stop], m - update], axis=0)
        after_panel(start // width)
    return [jnp.concatenate(rows, axis=0) for rows in done]


def factors(grams, after_panel):
    lane, sub = square_iotas()
    eye = jnp.where(lane == sub, 1.0, 0.0)
    full, one, two = [], [], []
    for m in eliminate(grams, 32, after_panel):
        diag = jnp.sum(jnp.where(lane == sub, m, 0.0), axis=1, keepdims=True)
        scale = lax.rsqrt(diag)
        f = scale * jnp.where(lane < sub, m, eye)
        upper = scale * jnp.where(lane >= sub, m, 0.0)
        fb = f.astype(BF16)
        second = eye + dotf(fb.astype(F32) - f, upper, ((1,), (1,)))
        second = jnp.where(lane <= sub, second, 0.0)
        full.append(f)
        one.append(fb)
        two.append(second)
    after_panel(V, one)
    powers = []
    same = lane // 16 == sub // 16
    for second in two:
        diag = jnp.sum(jnp.where(lane == sub, second, 0.0), axis=1, keepdims=True)
        powers.append((jnp.where(same & (lane < sub), second, 0.0) / diag, eye / diag))
    start = [p for _, p in powers]
    powers = [p for p, _ in powers]
    invs = [eye - p for p in powers]
    for _ in range(3):
        powers = [dotf(p, p, ((1,), (0,))) for p in powers]
        invs = [x + dotf(x, p, ((1,), (0,))) for x, p in zip(invs, powers)]
    invs = [dotf(x, d, ((1,), (0,))) for x, d in zip(invs, start)]
    s = 16
    while s < V:
        pick = (lane // (2 * s) == sub // (2 * s)) & (lane // s != sub // s) & (lane < sub)
        t = [dotf(jnp.where(pick, l2, 0.0), x, ((1,), (0,))) for l2, x in zip(two, invs)]
        invs = [x - dotf(x, y, ((1,), (0,))) for x, y in zip(invs, t)]
        s *= 2
    return full, one, invs


def pack(mats, ref):
    lane, sub = square_iotas()
    for p in range(K // 2):
        a, b = mats[2 * p], mats[2 * p + 1]
        both = jnp.where(sub >= lane, a, b).reshape(8, 16, V)
        ref[8 * p : 8 * p + 8, 0:16] = both
        ref[8 * p : 8 * p + 8, 16:17] = jnp.zeros((8, 1, V), F32)
        ref[8 * p, 16:17] = jnp.sum(jnp.where(sub == lane, b, 0.0), axis=0, keepdims=True)


def unpack(ref, scale):
    lane, sub = square_iotas()
    mats = []
    for p in range(K // 2):
        both = ref[8 * p : 8 * p + 8, 0:16].reshape(V, V) * scale
        turned = both.T
        diag = ref[8 * p, 16:17] * scale
        mats.append(jnp.where(sub >= lane, both, turned))
        mats.append(jnp.where(sub == lane, diag, jnp.where(sub < lane, both, turned)))
    return mats


class Summed:
    def __init__(self, refs, place):
        self.x, self.one, self.two, self.out = refs[:4]
        self.sems = refs[4:]
        self.place = place
        self.sent = []

    def copies(self, stage, count, source, target, device):
        send, recv = self.sems[2 * stage], self.sems[2 * stage + 1]
        made = [
            pltpu.make_async_remote_copy(
                src_ref=source(d),
                dst_ref=target(d),
                send_sem=send.at[d],
                recv_sem=recv.at[d],
                device_id=device(d)[1],
                device_id_type=MESH,
            )
            for d in range(1, count)
        ]
        for copy in made:
            copy.start()
        self.sent += made
        self.pending = made

    def arrived(self):
        for copy in self.pending:
            copy.wait_recv()

    def start_one(self):
        pl_ = self.place
        self.copies(0, pl_.plane, lambda d: self.x.at[pl_.in_plane(d)[0]], lambda d: self.one.at[d], pl_.in_plane)

    def start_two(self):
        self.arrived()
        pl_ = self.place
        total = self.x[pl_.me]
        for d in range(1, pl_.plane):
            total = total + self.one[d]
        self.two[pl_.a] = total
        self.copies(1, pl_.na, lambda d: self.two.at[pl_.a], lambda d: self.two.at[pl_.a], pl_.on_line)

    def start_three(self):
        self.arrived()
        pl_ = self.place
        total = self.two[0]
        for q in range(1, pl_.na):
            total = total + self.two[q]
        self.out[pl_.me] = total
        self.copies(2, pl_.plane, lambda d: self.out.at[pl_.me], lambda d: self.out.at[pl_.me], pl_.in_plane)

    def finish(self):
        self.arrived()

    def drain(self):
        for copy in self.sent:
            copy.wait_send()


class Place:
    def __init__(self):
        self.a, self.b, self.c = (lax.axis_index(n) for n in ("gx", "gy", "gz"))
        self.na, self.nb, self.nc = (lax.axis_size(n) for n in ("gx", "gy", "gz"))
        self.plane = self.nb * self.nc
        self.me = self.b * self.nc + self.c

    def in_plane(self, d):
        m = lax.rem(self.me + d, self.plane)
        return m, (self.a, m // self.nc, lax.rem(m, self.nc))

    def on_line(self, d):
        q = lax.rem(self.a + d, self.na)
        return q, (q, self.b, self.c)


def apply(rows, factor):
    return lax.dot_general(
        rows, factor, (((1,), (1,)), ((), ())), preferred_element_type=F32
    ).astype(BF16)


def project_kernel(cells, y_hbm, pot_hbm, gram_ref, red_ref, f2_ref, basis_hbm, image_hbm,
                   pad, app, base, zsend, zrecv, zlow, zhigh, potbuf, potpad, pott, load_sem, store_sem, halo_send, halo_recv, *sums):
    here = Place()
    a, b, c = here.a, here.b, here.c
    na, nb, nc = here.na, here.nb, here.nc
    first, second = Summed(sums[:10], here), Summed(sums[10:], here)

    loads = [
        pltpu.make_async_copy(y_hbm.at[k], pad.at[k, 1 : BX + 1, 1 : BY + 1], load_sem.at[k])
        for k in range(K)
    ]
    loads.append(pltpu.make_async_copy(pot_hbm, potbuf, load_sem.at[K]))
    for load in loads:
        load.start()

    barrier = pltpu.get_barrier_semaphore()
    for d in range(1, here.plane):
        pl.semaphore_signal(barrier, inc=1, device_id=here.in_plane(d)[1], device_id_type=MESH)
    for d in range(1, na):
        pl.semaphore_signal(barrier, inc=1, device_id=here.on_line(d)[1], device_id_type=MESH)

    @pl.when(a == 0)
    def _():
        pad[:, 0:1] = jnp.zeros((K, 1, BY + 2, BZ, V), BF16)

    @pl.when(a == na - 1)
    def _():
        pad[:, BX + 1 : BX + 2] = jnp.zeros((K, 1, BY + 2, BZ, V), BF16)

    @pl.when(b == 0)
    def _():
        pad[:, :, 0:1] = jnp.zeros((K, BX + 2, 1, BZ, V), BF16)

    @pl.when(b == nb - 1)
    def _():
        pad[:, :, BY + 1 : BY + 2] = jnp.zeros((K, BX + 2, 1, BZ, V), BF16)

    loads[K].wait()
    potpad[...] = jnp.zeros((V, V), F32)
    potpad[:, 0:BZ] = potbuf[...].reshape(V, BZ) + 6.0
    pott[...] = potpad[...].T[0:BZ]

    grams = []
    for k in range(K):
        loads[k].wait()
        rows = pad[k, 1 : BX + 1, 1 : BY + 1].reshape(BX * BY * BZ, V)
        grams.append(lax.dot_general(rows, rows, (((0,), (0,)), ((), ())), preferred_element_type=F32))
    pack(grams, first.x)

    def face(i, _):
        k, x = i // BX, lax.rem(i, BX)
        low = pad[k, x + 1, 1 : BY + 1, 0:16].astype(F32)[:, 0, :]
        high = pad[k, x + 1, 1 : BY + 1, 16:32].astype(F32)[:, 15, :]
        zsend[k, x] = jnp.where(c == 0, high, low).astype(BF16)
        return 0

    lax.fori_loop(0, K * BX, face, 0)

    pl.semaphore_wait(barrier, here.plane + na - 2)

    first.start_one()

    def halo(i, source, target, device):
        return [
            pltpu.make_async_remote_copy(
                src_ref=source(k),
                dst_ref=target(k),
                send_sem=halo_send.at[i, k],
                recv_sem=halo_recv.at[i, k],
                device_id=device,
                device_id_type=MESH,
            )
            for k in range(K)
        ]

    inner_y, inner_x = slice(1, BY + 1), slice(1, BX + 1)
    z_copy = halo(0, lambda k: zsend.at[k], lambda k: zrecv.at[k], (a, b, 1 - c))
    y_up = halo(
        1, lambda k: pad.at[k, inner_x, BY], lambda k: pad.at[k, inner_x, 0], (a, lax.rem(b + 1, nb), c)
    )
    y_down = halo(
        2, lambda k: pad.at[k, inner_x, 1], lambda k: pad.at[k, inner_x, BY + 1], (a, lax.rem(b + nb - 1, nb), c)
    )
    x_up = halo(
        3, lambda k: pad.at[k, BX, inner_y], lambda k: pad.at[k, 0, inner_y], (lax.rem(a + 1, na), b, c)
    )
    x_down = halo(
        4, lambda k: pad.at[k, 1, inner_y], lambda k: pad.at[k, BX + 1, inner_y], (lax.rem(a + na - 1, na), b, c)
    )

    def each(copies, what):
        def act():
            for copy in copies:
                getattr(copy, what)()

        return act

    each(z_copy, "start")()
    pl.when(b < nb - 1)(each(y_up, "start"))
    pl.when(b > 0)(each(y_down, "start"))

    each(z_copy, "wait_recv")()

    def spread(i, _):
        k, x = i // BX, lax.rem(i, BX)
        got = zrecv[k, x].astype(F32)
        zhigh[k, x] = jnp.where(c == 0, got, 0.0)
        zlow[k, x] = jnp.where(c == 0, 0.0, got)
        return 0

    lax.fori_loop(0, K * BX, spread, 0)
    zsub = lax.broadcasted_iota(jnp.int32, (BZ, V), 0)

    def cells_of(x, ys):
        columns = pltpu.roll(pott[...], lax.rem(V - x * BY, V), 1)
        for y in ys:
            weight = jnp.broadcast_to(columns[:, y : y + 1], (BZ, V))
            for k in range(K):
                center = pad[k, x + 1, y + 1].astype(F32)
                beside = pad[k, x + 2, y + 1].astype(F32) + pad[k, x, y + 1].astype(F32)
                beside = beside + pad[k, x + 1, y + 2].astype(F32)
                beside = beside + pad[k, x + 1, y].astype(F32)
                up = jnp.where(zsub == BZ - 1, zhigh[k, x, y : y + 1], pltpu.roll(center, BZ - 1, 0))
                down = jnp.where(zsub == 0, zlow[k, x, y : y + 1], pltpu.roll(center, 1, 0))
                app[k, x, y] = (weight * center - (beside + up + down)).astype(BF16)

    def planes(first_x, count, step, ys):
        def body(i, _):
            cells_of(first_x + i * step, ys)
            return 0

        lax.fori_loop(0, count, body, 0)

    planes(1, EARLY, 1, range(1, BY - 1))
    first.start_two()
    pl.when(a < na - 1)(each(x_up, "start"))
    pl.when(a > 0)(each(x_down, "start"))
    planes(1 + EARLY, BX - 2 - EARLY, 1, range(1, BY - 1))
    first.start_three()
    pl.when(b > 0)(each(y_up, "wait_recv"))
    pl.when(b < nb - 1)(each(y_down, "wait_recv"))
    planes(1, BX - 2, 1, (0, BY - 1))
    pl.when(a > 0)(each(x_up, "wait_recv"))
    pl.when(a < na - 1)(each(x_down, "wait_recv"))
    planes(0, 2, BX - 1, range(BY))

    crossed = []
    for k in range(K):
        rows = pad[k, 1 : BX + 1, 1 : BY + 1].reshape(BX * BY * BZ, V)
        image = app[k].reshape(BX * BY * BZ, V)
        part = lax.dot_general(rows, image, (((0,), (0,)), ((), ())), preferred_element_type=F32)
        crossed.append(part + part.T)
    pack(crossed, second.x)
    second.start_one()

    first.finish()
    grams = unpack(first.out, 1.0 / cells)
    for k in range(K):
        gram_ref[k] = grams[k]

    stores = []

    def between(i, one=None):
        if i == 2:
            second.start_two()
        if one is None:
            return
        for k in range(K):
            rows = pad[k, 1 : BX + 1, 1 : BY + 1].reshape(BX * BY * BZ, V)
            base[k] = apply(rows, one[k]).reshape(BX, BY, BZ, V)
            rows = app[k].reshape(BX * BY * BZ, V)
            app[k] = apply(rows, one[k]).reshape(BX, BY, BZ, V)
            for i, (source, target) in enumerate(((base, basis_hbm), (app, image_hbm))):
                stores.append(pltpu.make_async_copy(source.at[k], target.at[k], store_sem.at[i, k]))
                stores[-1].start()

    full, one, two = factors(grams, between)
    for k in range(K):
        f2_ref[k] = two[k].astype(BF16)
    second.start_three()
    second.finish()
    sides = unpack(second.out, 0.5 / cells)
    for k in range(K):
        half = dotf(full[k], sides[k], ((1,), (0,)))
        red_ref[k] = dotf(half, full[k], ((1,), (1,)))

    first.drain()
    second.drain()
    for store in stores:
        store.wait()
    each(z_copy, "wait_send")()
    pl.when(a < na - 1)(each(x_up, "wait_send"))
    pl.when(b < nb - 1)(each(y_up, "wait_send"))
    pl.when(a > 0)(each(x_down, "wait_send"))
    pl.when(b > 0)(each(y_down, "wait_send"))


def project(subspace, potential, cells):
    na, plane = lax.axis_size("gx"), lax.axis_size("gy") * lax.axis_size("gz")
    dma = pltpu.SemaphoreType.DMA
    vmem = pl.BlockSpec(memory_space=pltpu.VMEM)
    hbm = pl.BlockSpec(memory_space=pl.ANY)
    summed = [pltpu.VMEM((n, CHUNK, V), F32) for n in (plane, plane, na, plane)]
    summed += [dma((n,)) for n in (plane, plane, na, na, plane, plane)]
    square = jax.ShapeDtypeStruct((K, V, V), F32)
    narrow = jax.ShapeDtypeStruct((K, V, V), BF16)
    large = jax.ShapeDtypeStruct(subspace.shape, BF16)
    return pl.pallas_call(
        functools.partial(project_kernel, cells),
        out_shape=(square, square, narrow, large, large),
        in_specs=[hbm, pl.BlockSpec(memory_space=pltpu.HBM)],
        out_specs=(vmem, vmem, vmem, hbm, hbm),
        scratch_shapes=[
            pltpu.VMEM((K, BX + 2, BY + 2, BZ, V), BF16),
            pltpu.VMEM((K, BX, BY, BZ, V), BF16),
            pltpu.VMEM((K, BX, BY, BZ, V), BF16),
            pltpu.VMEM((K, BX, BY, V), BF16),
            pltpu.VMEM((K, BX, BY, V), BF16),
            pltpu.VMEM((K, BX, BY, V), F32),
            pltpu.VMEM((K, BX, BY, V), F32),
            pltpu.VMEM((BX, BY, BZ), F32),
            pltpu.VMEM((V, V), F32),
            pltpu.VMEM((BZ, V), F32),
            dma((K + 1,)),
            dma((2, K)),
            dma((5, K)),
            dma((5, K)),
        ]
        + summed
        + summed,
        compiler_params=pltpu.CompilerParams(
            collective_id=0, has_side_effects=True, vmem_limit_bytes=44 << 20
        ),
    )(subspace, potential)


def finish_kernel(y, image, f2, gram, red, y_out, image_out, gram_out, red_out):
    gram_out[...] = gram[...]
    red_out[...] = red[...]
    y_out[0] = apply(y[0], f2[0])
    image_out[0] = apply(image[0], f2[0])


def finish(y, image, f2, gram, red):
    rows = pl.BlockSpec((1, y.shape[1], V), lambda k: (k, 0, 0))
    square = pl.BlockSpec((1, V, V), lambda k: (k, 0, 0))
    small = jax.ShapeDtypeStruct((K, V, V), F32)
    large = jax.ShapeDtypeStruct(y.shape, BF16)
    return pl.pallas_call(
        finish_kernel,
        grid=(K,),
        in_specs=[rows, rows, square, square, square],
        out_specs=(rows, rows, square, square),
        out_shape=(large, large, small, small),
        compiler_params=pltpu.CompilerParams(vmem_limit_bytes=40 << 20),
    )(y, image, f2, gram, red)


def per_device(subspace, potential):
    cells = BX * BY * BZ * lax.axis_size("gx") * lax.axis_size("gy") * lax.axis_size("gz")
    gram, red, f2, basis, image = project(subspace, potential, cells)
    flat = (K, BX * BY * BZ, V)
    basis, image, gram, red = finish(
        basis.reshape(flat), image.reshape(flat), f2, gram, red
    )
    return basis.reshape(subspace.shape), image.reshape(subspace.shape), red, gram


def solution(mesh):
    return jax.shard_map(
        per_device,
        mesh=mesh,
        in_specs=(P(None, "gx", "gy", "gz", None), P("gx", "gy", "gz")),
        out_specs=(P(None, "gx", "gy", "gz", None), P(None, "gx", "gy", "gz", None), P(), P()),
        check_vma=False,
    )
```
